32 devices in a mesh: groups: 2 (over x), lon: 16 (over z, y, core).
Axes of the slice: x: 2, y: 2, z: 4, core: 2. Of those that a mesh axis runs over, the one named last changes fastest.
Arguments:
- fields: bfloat16 [64, 32, 4096], P('groups', 'lon'), parts along dimension 0, may hold values from -6 to 6
- couplings: bfloat16 [32, 9, 64, 64], replicated, may hold values from -0.25 to 0.25
- kappa: float32 [64, 32, 64], P('groups', 'lon'), parts along dimension 0, may hold values from -1 to 1
- coeffs: float32 [3], replicated, may hold values from 0.3 to 1
- foot_lat: int32 [1024, 4], P(('groups', 'lon')), parts along dimension 0, may hold values from 0 to 31
- foot_lon: int32 [1024, 4], P(('groups', 'lon')), parts along dimension 0, may hold values from 0 to 3
- foot_w: bfloat16 [4, 64, 64], replicated, may hold values from -0.375 to 0.375
- thresholds: float32 [16], replicated, may hold values from -2 to 2
- bins: int32 [1024], P(('groups', 'lon')), parts along dimension 0, may hold values from 0 to 15
Outputs:
- filtered: bfloat16 [64, 32, 4096], P('groups', 'lon'), parts along dimension 0
- score: float32 [1024, 64], P(('groups', 'lon')), parts along dimension 0
- summary: float32 [32], P('groups'), parts along dimension 0
The draws below stay inside these ranges and needn't reach their ends.
There are 2 independent parts, one for each index of `groups`. The reference program is written for one: setup_inputs(seed, part) draws one part's arguments, and reference() takes and returns one part's arrays. A program takes and returns all parts, laid end to end along the dimension named above; an argument that names none is the same for every part. Nothing has to cross between parts.
All inputs are finite; a program needn't handle non-finite values.
Results may differ from the reference program's by a relative error of at most 0.014.
Values may be sent and summed in bfloat16 or wider, within the bound.
A program may use at most 128 MiB of HBM per device.

```python
import jax
import jax.numpy as jnp

BN = 64
R = 64
NLAT = 32
LB = 2
K = 4
NOBS_DEV = 32
NBINS = 16
NLON = 32
NOBS = 512


def place_ends(entries, own_key, smallest, top_value):
    dims = entries.shape
    place = [jax.random.randint(jax.random.fold_in(own_key, axis), (), 0, dims[axis]) for axis in range(len(dims))]
    entries = entries.at[tuple(place)].set(smallest)
    longest = dims.index(max(dims))
    place[longest] = (place[longest] + 1) % dims[longest]
    return entries.at[tuple(place)].set(top_value)


def level_of(stream_key, dims, split, least, largest):
    factor_of = 1.0
    for dim, shards_of in split:
        draws = jax.random.uniform(jax.random.fold_in(jax.random.fold_in(stream_key, 6), dim), (shards_of,), jnp.float32, least / len(split), largest / len(split))
        factor_of = factor_of * jnp.repeat(jnp.exp(draws), dims[dim] // shards_of).reshape((-1,) + (1,) * (len(dims) - 1 - dim))
    return factor_of


def bell_draw(rng, dims, spread, reach, split=(), kind=jnp.bfloat16):
    values = jax.random.normal(rng, dims, jnp.float32) * spread
    if len(split) > 0:
        values = level_of(rng, dims, split, -0.22, 0.18) * values
    return jnp.clip(values, min=-reach, max=reach).astype(kind)


def setup_inputs(seed: int = 0, part: int = 0) -> dict:
    key_of = jax.random.split(jax.random.key(seed), 10)
    part_keys = jax.random.split(jax.random.fold_in(key_of[9], part), 10)
    return {
        "fields": bell_draw(part_keys[0], (NLAT, NLON, BN * R), 1.0, 6.0, ((1, 16),)),
        "couplings": bell_draw(key_of[1], (NLAT, 9, BN, BN), (9 * BN) ** -0.5, 0.25),
        "kappa": jnp.clip(jax.random.uniform(part_keys[2], (NLAT, NLON, BN), jnp.float32, -1.0, 1.0) * level_of(part_keys[2], (NLAT, NLON, BN), ((1, 16),), -0.4, 0.0), -1.0, 1.0),
        "coeffs": jnp.clip(jax.random.uniform(key_of[3], (3,), jnp.float32, 0.3, 1.0), 0.3, 1.0),
        "foot_lat": place_ends(jax.random.randint(part_keys[4], (NOBS, K), 0, NLAT), jax.random.fold_in(part_keys[4], 1), 0, NLAT - 1).astype(jnp.int32),
        "foot_lon": place_ends(jax.random.randint(part_keys[5], (NOBS, K), 0, 2 * LB), jax.random.fold_in(part_keys[5], 1), 0, (2 * LB) - 1).astype(jnp.int32),
        "foot_w": bell_draw(key_of[6], (K, BN, BN), (K * BN) ** -0.5, 0.375),
        "thresholds": jnp.clip(jax.random.uniform(key_of[7], (NBINS,), jnp.float32, -2.0, 2.0), -2.0, 2.0),
        "bins": place_ends(jax.random.randint(part_keys[8], (NOBS,), 0, NBINS), jax.random.fold_in(part_keys[8], 1), 0, NBINS - 1).astype(jnp.int32),
    }


tau_width = 0.5


def apply_op(v, couplings, kappa):
    padded = jnp.pad(v, ((1, 1), (0, 0), (0, 0), (0, 0)))
    padded = jnp.concatenate([padded[:, -1:], padded, padded[:, :1]], axis=1)
    nlat = v.shape[0]
    nlon = v.shape[1]
    total = kappa[..., None] * v.astype(jnp.float32)
    for row_off in range(3):
        for col_off in range(3):
            piece = padded[row_off:row_off + nlat, col_off:col_off + nlon].astype(jnp.float32)
            coup = couplings[:, 3 * row_off + col_off].astype(jnp.float32)
            total = total + jnp.einsum('iab,ijbr->ijar', coup, piece)
    return total


def reference(fields, couplings, kappa, coeffs, foot_lat, foot_lon, foot_w, thresholds, bins):
    start = fields.reshape(NLAT, NLON, BN, R)
    term_one = apply_op(start, couplings, kappa).astype(jnp.bfloat16)
    term_two = 2.0 * apply_op(term_one, couplings, kappa) - start.astype(jnp.float32)
    filtered = (coeffs[0] * start.astype(jnp.float32) + coeffs[1] * term_one.astype(jnp.float32) + coeffs[2] * term_two).astype(jnp.bfloat16)
    owner = (jnp.arange(NOBS, dtype=jnp.int32) // NOBS_DEV).astype(jnp.int32)
    lon_block = (owner[:, None] * LB + foot_lon) % NLON
    blocks = filtered[foot_lat, lon_block].astype(jnp.float32)
    observed = jnp.einsum('kab,fkbr->far', foot_w.astype(jnp.float32), blocks)
    onehot = (bins[:, None] == jnp.arange(NBINS, dtype=jnp.int32)[None, :]).astype(jnp.float32)
    level = jnp.sum(onehot * thresholds[None, :], axis=1)
    ecdf = jnp.mean(jax.nn.sigmoid((level[:, None, None] - observed) / tau_width), axis=2)
    totals = jnp.sum(onehot * jnp.sum(ecdf, axis=1)[:, None], axis=0)
    counts = jnp.sum(onehot, axis=0) * BN
    summary = totals / jnp.maximum(counts, 1.0)
    score = ecdf - jnp.sum(onehot * summary[None, :], axis=1)[:, None]
    return filtered.reshape(NLAT, NLON, BN * R), score, summary
```

```python
import functools

import jax
import jax.numpy as jnp
from jax import lax
from jax.experimental import pallas as pl
from jax.experimental.pallas import tpu as pltpu
from jax.sharding import PartitionSpec as P

MESH = pl.DeviceIdType.MESH
F32 = jnp.float32
BF16 = jnp.bfloat16
tau_width = 0.5
LANES = 128


def kernel(n, nlat, nb, nobs, nk, nbins, nch, *refs):
    (x_ref, kt_ref, coup_hbm, foot_w_ref, binscol_ref, coef_ref, lat_ref, lon_ref, thr_ref, bins_ref,
     filt_ref, score_ref, summ_ref,
     xw, xo, xe, kw, ke, coup, wc, kx, t1, feast, fb, ecdf, msg, inbox,
     xs_sem, xr_sem, ks_sem, kr_sem, c_sem, fs_sem, fr_sem, ms_sem, mr_sem) = refs
    me = lax.axis_index("lon")
    east, west = lax.rem(me + 1, n), lax.rem(me + n - 1, n)
    ch = nlat // nch
    w2 = 2 * nb

    barrier = pltpu.get_barrier_semaphore()

    def greet(off, carry):
        pl.semaphore_signal(barrier, inc=1, device_id={"lon": lax.rem(me + off, n)}, device_id_type=MESH)
        return carry

    lax.fori_loop(1, n, greet, 0)
    c_copy = pltpu.make_async_copy(coup_hbm, coup, c_sem)
    c_copy.start()
    pl.semaphore_wait(barrier, n - 1)

    kcopies = []
    for side, (dst, dev) in enumerate(((kw, east), (ke, west))):
        cp = pltpu.make_async_remote_copy(
            src_ref=kt_ref, dst_ref=dst, send_sem=ks_sem.at[side], recv_sem=kr_sem.at[side],
            device_id={"lon": dev}, device_id_type=MESH)
        cp.start()
        kcopies.append(cp)
    xcopies = []
    for c in range(nch):
        pair = []
        for side, (dst, dev) in enumerate(((xw, east), (xe, west))):
            cp = pltpu.make_async_remote_copy(
                src_ref=x_ref.at[pl.ds(c * ch, ch)], dst_ref=dst.at[pl.ds(1 + c * ch, ch)],
                send_sem=xs_sem.at[side, c], recv_sem=xr_sem.at[side, c],
                device_id={"lon": dev}, device_id_type=MESH)
            cp.start()
            pair.append(cp)
        xcopies.append(pair)

    zero = jnp.zeros((nb, w2), BF16)
    for buf in (xw, xo, xe):
        buf[0] = zero
        buf[nlat + 1] = zero
    t1[0] = jnp.zeros((nb, 2 * w2), BF16)
    t1[nlat + 1] = jnp.zeros((nb, 2 * w2), BF16)
    xo[pl.ds(1, nlat)] = x_ref[...]

    c_copy.wait()

    def widen(i, carry):
        wc[i] = jnp.concatenate(
            [coup[i, pl.ds(3 * a, 3)].reshape(3 * nb, nb) for a in range(3)], axis=1)
        return carry

    lax.fori_loop(0, nlat, widen, 0, unroll=2)

    for cp in kcopies:
        cp.wait()
    kwv, kov, kev = kw[...], kt_ref[...], ke[...]
    low = lax.broadcasted_iota(jnp.int32, (nb, w2), 1) < nb

    def spread(v, j):
        return jnp.broadcast_to(v[:, j:j + 1], (nb, w2))

    for i in range(nlat):
        kx[i, :, 0:w2] = spread(kwv, 2 * i + 1)
        kx[i, :, w2:2 * w2] = jnp.where(low, spread(kov, 2 * i), spread(kov, 2 * i + 1))
        kx[i, :, 2 * w2:3 * w2] = spread(kev, 2 * i)

    c0, c1, c2 = coef_ref[0], coef_ref[1], coef_ref[2]

    def first(i, carry):
        rhs = jnp.concatenate(
            [buf[pl.ds(i, 3)].reshape(3 * nb, w2) for buf in (xw, xo, xe)], axis=1)
        p = jnp.dot(wc[i], rhs, preferred_element_type=F32)
        centre = jnp.concatenate([buf[i + 1].astype(F32) for buf in (xw, xo, xe)], axis=1)
        mid = p[nb:2 * nb] + kx[i] * centre
        total = p[0:nb, 0:2 * w2] + p[2 * nb:3 * nb, w2:3 * w2] + mid[:, nb:nb + 2 * w2]
        t1[i + 1] = total.astype(BF16)
        return carry

    def second(i, carry):
        p = jnp.dot(wc[i], t1[pl.ds(i, 3)].reshape(3 * nb, 2 * w2), preferred_element_type=F32)
        own = t1[i + 1].astype(F32)[:, nb:nb + w2]
        st = (p[0:nb, 0:w2] + p[2 * nb:3 * nb, w2:2 * w2] + p[nb:2 * nb, nb:nb + w2]
              + kx[i, :, w2:2 * w2] * own)
        x = x_ref[i].astype(F32)
        f = (c0 * x + c1 * own + c2 * (2.0 * st - x)).astype(BF16)
        filt_ref[i] = f
        fb[2 * i] = f[:, 0:nb]
        fb[2 * i + 1] = f[:, nb:w2]
        return carry

    fcopies = []
    for c in range(nch):
        for cp in xcopies[c]:
            cp.wait_recv()
        last = c == nch - 1
        t_lo, t_hi = max(c * ch - 1, 0), nlat if last else (c + 1) * ch - 1
        f_lo, f_hi = max(c * ch - 2, 0), nlat if last else (c + 1) * ch - 2
        lax.fori_loop(t_lo, t_hi, first, 0, unroll=2)
        lax.fori_loop(f_lo, f_hi, second, 0, unroll=2)
        cp = pltpu.make_async_remote_copy(
            src_ref=filt_ref.at[pl.ds(f_lo, f_hi - f_lo)], dst_ref=feast.at[pl.ds(f_lo, f_hi - f_lo)],
            send_sem=fs_sem.at[c], recv_sem=fr_sem.at[c],
            device_id={"lon": west}, device_id_type=MESH)
        cp.start()
        fcopies.append((cp, f_lo, f_hi))

    def unpack(i, carry):
        f = feast[i]
        fb[2 * (nlat + i)] = f[:, 0:nb]
        fb[2 * (nlat + i) + 1] = f[:, nb:w2]
        return carry

    for cp, f_lo, f_hi in fcopies:
        cp.wait_recv()
        lax.fori_loop(f_lo, f_hi, unpack, 0, unroll=2)

    ones = jnp.ones((8, nb), BF16)
    nt = (((1,), (1,)), ((), ()))

    def foot(f, carry):
        picks = []
        for k in range(nk):
            la, lo = lat_ref[f, k], lon_ref[f, k]
            picks.append(fb[(lo // 2) * (2 * nlat) + 2 * la + lo % 2])
        y = jnp.dot(foot_w_ref[...], jnp.concatenate(picks, axis=0), preferred_element_type=F32)
        s = jnp.tanh((thr_ref[bins_ref[f]] - y) * (0.5 / tau_width))
        hi = s.astype(BF16)
        lo_part = (s - hi.astype(F32)).astype(BF16)
        row = (lax.dot_general(ones, hi, nt, preferred_element_type=F32)
               + lax.dot_general(ones, lo_part, nt, preferred_element_type=F32))
        ecdf[pl.ds(f, 1)] = 0.5 + (0.5 / nb) * row[0:1]
        return carry

    lax.fori_loop(0, nobs, foot, 0, unroll=4)

    onehot = (binscol_ref[...] == lax.broadcasted_iota(jnp.int32, (nobs, LANES), 1)).astype(F32)
    ec = ecdf[...]
    totals = jnp.sum(onehot * jnp.sum(ec, axis=1, keepdims=True), axis=0, keepdims=True)
    counts = jnp.sum(onehot, axis=0, keepdims=True) * nb
    msg[0:1] = totals
    msg[1:2] = counts
    msg[2:8] = jnp.zeros((6, LANES), F32)
    inbox[pl.ds(me, 1)] = msg[...][None]

    def tell(off, carry):
        pltpu.make_async_remote_copy(
            src_ref=msg, dst_ref=inbox.at[me], send_sem=ms_sem.at[off], recv_sem=mr_sem.at[me],
            device_id={"lon": lax.rem(me + off, n)}, device_id_type=MESH).start()
        return carry

    lax.fori_loop(1, n, tell, 0)

    def hear(off, carry):
        src = lax.rem(me + off, n)
        pltpu.make_async_remote_copy(
            src_ref=msg, dst_ref=inbox.at[src], send_sem=ms_sem.at[off], recv_sem=mr_sem.at[src],
            device_id={"lon": src}, device_id_type=MESH).wait()
        return carry

    lax.fori_loop(1, n, hear, 0)
    allsum = jnp.sum(inbox[...], axis=0)
    summary = allsum[0:1] / jnp.maximum(allsum[1:2], 1.0)
    summ_ref[...] = summary
    score_ref[...] = ec - jnp.sum(onehot * summary, axis=1, keepdims=True)

    for pair in xcopies:
        for cp in pair:
            cp.wait_send()
    for cp, _, _ in fcopies:
        cp.wait_send()


def local(n, fields, couplings, kappa, coeffs, foot_lat, foot_lon, foot_w, thresholds, bins):
    nlat, width = fields.shape[0], fields.shape[1]
    nb = couplings.shape[-1]
    nobs, nk = foot_lat.shape
    nbins = thresholds.shape[0]
    w2 = 2 * nb
    nch = 4
    x = fields.reshape(nlat, width, nb, nb).transpose(0, 2, 1, 3).reshape(nlat, nb, w2)
    kt = kappa.reshape(nlat * width, nb).T
    fw = foot_w.transpose(1, 0, 2).reshape(nb, nk * nb)
    vmem = pl.BlockSpec(memory_space=pltpu.VMEM)
    smem = pl.BlockSpec(memory_space=pltpu.SMEM)
    hbm = pl.BlockSpec(memory_space=pl.ANY)
    dma = pltpu.SemaphoreType.DMA
    filt, score, summ = pl.pallas_call(
        functools.partial(kernel, n, nlat, nb, nobs, nk, nbins, nch),
        out_shape=(
            jax.ShapeDtypeStruct((nlat, nb, w2), BF16),
            jax.ShapeDtypeStruct((nobs, nb), F32),
            jax.ShapeDtypeStruct((1, LANES), F32),
        ),
        in_specs=[vmem, vmem, hbm, vmem, vmem, smem, smem, smem, smem, smem],
        out_specs=(vmem, vmem, vmem),
        scratch_shapes=[
            pltpu.VMEM((nlat + 2, nb, w2), BF16),
            pltpu.VMEM((nlat + 2, nb, w2), BF16),
            pltpu.VMEM((nlat + 2, nb, w2), BF16),
            pltpu.VMEM((nb, nlat * width), F32),
            pltpu.VMEM((nb, nlat * width), F32),
            pltpu.VMEM(couplings.shape, BF16),
            pltpu.VMEM((nlat, 3 * nb, 3 * nb), BF16),
            pltpu.VMEM((nlat, nb, 3 * w2), F32),
            pltpu.VMEM((nlat + 2, nb, 2 * w2), BF16),
            pltpu.VMEM((nlat, nb, w2), BF16),
            pltpu.VMEM((4 * nlat, nb, nb), BF16),
            pltpu.VMEM((nobs, nb), F32),
            pltpu.VMEM((8, LANES), F32),
            pltpu.VMEM((n, 8, LANES), F32),
            dma((2, nch)), dma((2, nch)), dma((2,)), dma((2,)), dma,
            dma((nch,)), dma((nch,)), dma((n,)), dma((n,)),
        ],
        compiler_params=pltpu.CompilerParams(
            collective_id=0, has_side_effects=True, vmem_limit_bytes=40 * 1024 * 1024),
    )(x, kt, couplings, fw, bins[:, None], coeffs, foot_lat, foot_lon, thresholds, bins)
    filtered = filt.reshape(nlat, nb, width, nb).transpose(0, 2, 1, 3).reshape(nlat, width, nb * nb)
    return filtered, score, summ[0, :nbins]


def solution(mesh):
    placed = (
        P("groups", "lon", None),
        P(),
        P("groups", "lon", None),
        P(),
        P(("groups", "lon"), None),
        P(("groups", "lon"), None),
        P(),
        P(),
        P(("groups", "lon")),
    )
    return jax.shard_map(
        functools.partial(local, mesh.shape["lon"]),
        mesh=mesh,
        in_specs=placed,
        out_specs=(P("groups", "lon", None), P(("groups", "lon"), None), P("groups")),
        check_vma=False,
    )
```

```python
import functools

import jax
import jax.numpy as jnp
from jax import lax
from jax.experimental import pallas as pl
from jax.experimental.pallas import tpu as pltpu
from jax.sharding import PartitionSpec as P

MESH = pl.DeviceIdType.MESH
F32 = jnp.float32
BF16 = jnp.bfloat16
tau_width = 0.5
LANES = 128


def kernel(n, nlat, nb, nobs, nk, nbins, nch, *refs):
    (x_ref, kt_ref, coup_hbm, foot_w_ref, binscol_ref, coef_ref, lat_ref, lon_ref, thr_ref, bins_ref,
     filt_ref, score_ref, summ_ref,
     xw, xe, xc, kw, ke, coup, wc, kx, t1, fown, feast, fb, ecdf, msg, inbox,
     xs_sem, xr_sem, ks_sem, kr_sem, c_sem, fs_sem, fr_sem, ms_sem, mr_sem) = refs
    me = lax.axis_index("lon")
    east, west = lax.rem(me + 1, n), lax.rem(me + n - 1, n)
    ch = nlat // nch
    w2 = 2 * nb

    barrier = pltpu.get_barrier_semaphore()

    def greet(off, carry):
        pl.semaphore_signal(barrier, inc=1, device_id={"lon": lax.rem(me + off, n)}, device_id_type=MESH)
        return carry

    lax.fori_loop(1, n, greet, 0)
    c_copy = pltpu.make_async_copy(coup_hbm, coup, c_sem)
    c_copy.start()
    pl.semaphore_wait(barrier, n - 1)

    kcopies = []
    for side, (dst, dev) in enumerate(((kw, east), (ke, west))):
        cp = pltpu.make_async_remote_copy(
            src_ref=kt_ref, dst_ref=dst, send_sem=ks_sem.at[side], recv_sem=kr_sem.at[side],
            device_id={"lon": dev}, device_id_type=MESH)
        cp.start()
        kcopies.append(cp)
    xcopies = []
    for c in range(nch):
        pair = []
        for side, (dst, dev) in enumerate(((xw, east), (xe, west))):
            cp = pltpu.make_async_remote_copy(
                src_ref=x_ref.at[pl.ds(c * ch, ch)], dst_ref=dst.at[pl.ds(c * ch, ch)],
                send_sem=xs_sem.at[side, c], recv_sem=xr_sem.at[side, c],
                device_id={"lon": dev}, device_id_type=MESH)
            cp.start()
            pair.append(cp)
        xcopies.append(pair)

    xc[0] = jnp.zeros((nb, 3 * w2), BF16)
    xc[nlat + 1] = jnp.zeros((nb, 3 * w2), BF16)
    t1[0] = jnp.zeros((nb, 2 * w2), BF16)
    t1[nlat + 1] = jnp.zeros((nb, 2 * w2), BF16)

    rows = lax.broadcasted_iota(jnp.int32, (nb, nb), 0)
    cols = lax.broadcasted_iota(jnp.int32, (nb, nb), 1)
    swap = (rows + 1 - 2 * (rows % 2) == cols).astype(F32).astype(BF16)
    lane_hi = (lax.broadcasted_iota(jnp.int32, (nb, w2), 1) >= nb).astype(jnp.int32)
    keep = lax.broadcasted_iota(jnp.int32, (nb, w2), 0) % 2 == lane_hi

    def turned(v):
        other = jnp.dot(swap, v, preferred_element_type=F32)
        return jnp.where(keep, v.astype(F32), pltpu.roll(other, nb, 1)).astype(BF16)

    def turn_own(i, carry):
        xc[i + 1, :, w2:2 * w2] = turned(x_ref[i])
        return carry

    lax.fori_loop(0, nlat, turn_own, 0, unroll=4)

    def turn_sides(i, carry):
        xc[i + 1, :, 0:w2] = turned(xw[i])
        xc[i + 1, :, 2 * w2:3 * w2] = turned(xe[i])
        return carry

    c_copy.wait()

    def widen(i, carry):
        wc[i] = jnp.concatenate(
            [coup[i, pl.ds(3 * a, 3)].reshape(3 * nb, nb) for a in range(3)], axis=1)
        return carry

    lax.fori_loop(0, nlat, widen, 0, unroll=2)

    for cp in kcopies:
        cp.wait()
    kwv, kov, kev = kw[...], kt_ref[...], ke[...]
    low = lax.broadcasted_iota(jnp.int32, (nb, w2), 1) < nb

    def spread(v, j):
        return jnp.broadcast_to(v[:, j:j + 1], (nb, w2))

    for i in range(nlat):
        kx[i, :, 0:w2] = spread(kwv, 2 * i + 1)
        kx[i, :, w2:2 * w2] = jnp.where(low, spread(kov, 2 * i), spread(kov, 2 * i + 1))
        kx[i, :, 2 * w2:3 * w2] = spread(kev, 2 * i)

    c0, c1, c2 = coef_ref[0], coef_ref[1], coef_ref[2]

    def first(i, carry):
        p = jnp.dot(wc[i], xc[pl.ds(i, 3)].reshape(3 * nb, 3 * w2), preferred_element_type=F32)
        centre = xc[i + 1].astype(F32)
        mid = p[nb:2 * nb] + kx[i] * centre
        total = p[0:nb, 0:2 * w2] + p[2 * nb:3 * nb, w2:3 * w2] + mid[:, nb:nb + 2 * w2]
        t1[i + 1] = total.astype(BF16)
        return carry

    def second(i, carry):
        p = jnp.dot(wc[i], t1[pl.ds(i, 3)].reshape(3 * nb, 2 * w2), preferred_element_type=F32)
        own = t1[i + 1].astype(F32)[:, nb:nb + w2]
        st = (p[0:nb, 0:w2] + p[2 * nb:3 * nb, w2:2 * w2] + p[nb:2 * nb, nb:nb + w2]
              + kx[i, :, w2:2 * w2] * own)
        x = xc[i + 1, :, w2:2 * w2].astype(F32)
        f = (c0 * x + c1 * own + c2 * (2.0 * st - x)).astype(BF16)
        fown[i] = f
        fb[2 * i] = f[:, 0:nb]
        fb[2 * i + 1] = f[:, nb:w2]
        return carry

    fcopies = []
    for c in range(nch):
        for cp in xcopies[c]:
            cp.wait_recv()
        last = c == nch - 1
        t_lo, t_hi = max(c * ch - 1, 0), nlat if last else (c + 1) * ch - 1
        f_lo, f_hi = max(c * ch - 2, 0), nlat if last else (c + 1) * ch - 2
        lax.fori_loop(c * ch, (c + 1) * ch, turn_sides, 0, unroll=2)
        lax.fori_loop(t_lo, t_hi, first, 0, unroll=2)
        lax.fori_loop(f_lo, f_hi, second, 0, unroll=2)
        cp = pltpu.make_async_remote_copy(
            src_ref=fown.at[pl.ds(f_lo, f_hi - f_lo)], dst_ref=feast.at[pl.ds(f_lo, f_hi - f_lo)],
            send_sem=fs_sem.at[c], recv_sem=fr_sem.at[c],
            device_id={"lon": west}, device_id_type=MESH)
        cp.start()
        fcopies.append((cp, f_lo, f_hi))

    def turn_out(i, carry):
        filt_ref[i] = turned(fown[i])
        return carry

    lax.fori_loop(0, nlat, turn_out, 0, unroll=4)

    def unpack(i, carry):
        f = feast[i]
        fb[2 * (nlat + i)] = f[:, 0:nb]
        fb[2 * (nlat + i) + 1] = f[:, nb:w2]
        return carry

    for cp, f_lo, f_hi in fcopies:
        cp.wait_recv()
        lax.fori_loop(f_lo, f_hi, unpack, 0, unroll=2)

    ones = jnp.ones((8, nb), BF16)
    nt = (((1,), (1,)), ((), ()))

    def foot(f, carry):
        picks = []
        for k in range(nk):
            la, lo = lat_ref[f, k], lon_ref[f, k]
            picks.append(fb[(lo // 2) * (2 * nlat) + 2 * la + lo % 2])
        y = jnp.dot(foot_w_ref[...], jnp.concatenate(picks, axis=0), preferred_element_type=F32)
        s = jnp.tanh((thr_ref[bins_ref[f]] - y) * (0.5 / tau_width))
        hi = s.astype(BF16)
        lo_part = (s - hi.astype(F32)).astype(BF16)
        row = (lax.dot_general(ones, hi, nt, preferred_element_type=F32)
               + lax.dot_general(ones, lo_part, nt, preferred_element_type=F32))
        ecdf[pl.ds(f, 1)] = 0.5 + (0.5 / nb) * row[0:1]
        return carry

    lax.fori_loop(0, nobs, foot, 0, unroll=4)

    onehot = (binscol_ref[...] == lax.broadcasted_iota(jnp.int32, (nobs, LANES), 1)).astype(F32)
    ec = ecdf[...]
    totals = jnp.sum(onehot * jnp.sum(ec, axis=1, keepdims=True), axis=0, keepdims=True)
    counts = jnp.sum(onehot, axis=0, keepdims=True) * nb
    msg[0:1] = totals
    msg[1:2] = counts
    msg[2:8] = jnp.zeros((6, LANES), F32)
    inbox[pl.ds(me, 1)] = msg[...][None]

    def tell(off, carry):
        pltpu.make_async_remote_copy(
            src_ref=msg, dst_ref=inbox.at[me], send_sem=ms_sem.at[off], recv_sem=mr_sem.at[me],
            device_id={"lon": lax.rem(me + off, n)}, device_id_type=MESH).start()
        return carry

    lax.fori_loop(1, n, tell, 0)

    def hear(off, carry):
        src = lax.rem(me + off, n)
        pltpu.make_async_remote_copy(
            src_ref=msg, dst_ref=inbox.at[src], send_sem=ms_sem.at[off], recv_sem=mr_sem.at[src],
            device_id={"lon": src}, device_id_type=MESH).wait()
        return carry

    lax.fori_loop(1, n, hear, 0)
    allsum = jnp.sum(inbox[...], axis=0)
    summary = allsum[0:1] / jnp.maximum(allsum[1:2], 1.0)
    summ_ref[...] = summary
    score_ref[...] = ec - jnp.sum(onehot * summary, axis=1, keepdims=True)

    for pair in xcopies:
        for cp in pair:
            cp.wait_send()
    for cp, _, _ in fcopies:
        cp.wait_send()


def local(n, fields, couplings, kappa, coeffs, foot_lat, foot_lon, foot_w, thresholds, bins):
    nlat, width = fields.shape[0], fields.shape[1]
    nb = couplings.shape[-1]
    nobs, nk = foot_lat.shape
    nbins = thresholds.shape[0]
    w2 = 2 * nb
    nch = 4
    halves = nb * nb // w2
    x = fields.reshape(nlat, width, halves, w2).transpose(0, 2, 1, 3).reshape(nlat, nb, w2)
    kt = kappa.reshape(nlat * width, nb).T
    fw = foot_w.transpose(1, 0, 2).reshape(nb, nk * nb)
    vmem = pl.BlockSpec(memory_space=pltpu.VMEM)
    smem = pl.BlockSpec(memory_space=pltpu.SMEM)
    hbm = pl.BlockSpec(memory_space=pltpu.HBM)
    dma = pltpu.SemaphoreType.DMA
    filt, score, summ = pl.pallas_call(
        functools.partial(kernel, n, nlat, nb, nobs, nk, nbins, nch),
        out_shape=(
            jax.ShapeDtypeStruct((nlat, nb, w2), BF16),
            jax.ShapeDtypeStruct((nobs, nb), F32),
            jax.ShapeDtypeStruct((1, LANES), F32),
        ),
        in_specs=[vmem, vmem, hbm, vmem, vmem, smem, smem, smem, smem, smem],
        out_specs=(vmem, vmem, vmem),
        scratch_shapes=[
            pltpu.VMEM((nlat, nb, w2), BF16),
            pltpu.VMEM((nlat, nb, w2), BF16),
            pltpu.VMEM((nlat + 2, nb, 3 * w2), BF16),
            pltpu.VMEM((nb, nlat * width), F32),
            pltpu.VMEM((nb, nlat * width), F32),
            pltpu.VMEM(couplings.shape, BF16),
            pltpu.VMEM((nlat, 3 * nb, 3 * nb), BF16),
            pltpu.VMEM((nlat, nb, 3 * w2), F32),
            pltpu.VMEM((nlat + 2, nb, 2 * w2), BF16),
            pltpu.VMEM((nlat, nb, w2), BF16),
            pltpu.VMEM((nlat, nb, w2), BF16),
            pltpu.VMEM((4 * nlat, nb, nb), BF16),
            pltpu.VMEM((nobs, nb), F32),
            pltpu.VMEM((8, LANES), F32),
            pltpu.VMEM((n, 8, LANES), F32),
            dma((2, nch)), dma((2, nch)), dma((2,)), dma((2,)), dma,
            dma((nch,)), dma((nch,)), dma((n,)), dma((n,)),
        ],
        compiler_params=pltpu.CompilerParams(
            collective_id=0, has_side_effects=True, vmem_limit_bytes=60 * 1024 * 1024),
    )(x, kt, couplings, fw, bins[:, None], coeffs, foot_lat, foot_lon, thresholds, bins)
    filtered = filt.reshape(nlat, halves, width, w2).transpose(0, 2, 1, 3).reshape(nlat, width, nb * nb)
    return filtered, score, summ[0, :nbins]


def solution(mesh):
    placed = (
        P("groups", "lon", None),
        P(),
        P("groups", "lon", None),
        P(),
        P(("groups", "lon"), None),
        P(("groups", "lon"), None),
        P(),
        P(),
        P(("groups", "lon")),
    )
    return jax.shard_map(
        functools.partial(local, mesh.shape["lon"]),
        mesh=mesh,
        in_specs=placed,
        out_specs=(P("groups", "lon", None), P(("groups", "lon"), None), P("groups")),
        check_vma=False,
    )
```

```python
import functools

import jax
import jax.numpy as jnp
from jax import lax
from jax.experimental import pallas as pl
from jax.experimental.pallas import tpu as pltpu
from jax.sharding import PartitionSpec as P

MESH = pl.DeviceIdType.MESH
F32 = jnp.float32
BF16 = jnp.bfloat16
tau_width = 0.5
LANES = 128


def kernel(n, nlat, nb, nobs, nk, nbins, nch, *refs):
    (x_ref, kt_ref, coup_hbm, foot_w_ref, coef_ref, lat_ref, lon_ref, thr_ref, bins_ref,
     filt_ref, score_ref, summ_ref,
     xw, xe, xc, kw, ke, coup, wc, kx, t1, fown, feast, fb, fw, hot, ecdf, msg, inbox,
     xs_sem, xr_sem, ks_sem, kr_sem, c_sem, fs_sem, fr_sem, ms_sem, mr_sem) = refs
    me = lax.axis_index("lon")
    east, west = lax.rem(me + 1, n), lax.rem(me + n - 1, n)
    ch = nlat // nch
    w2 = 2 * nb

    barrier = pltpu.get_barrier_semaphore()

    def greet(off, carry):
        pl.semaphore_signal(barrier, inc=1, device_id={"lon": lax.rem(me + off, n)}, device_id_type=MESH)
        return carry

    lax.fori_loop(1, n, greet, 0)
    c_copy = pltpu.make_async_copy(coup_hbm, coup, c_sem)
    c_copy.start()
    pl.semaphore_wait(barrier, n - 1)

    kcopies = []
    for side, (dst, dev) in enumerate(((kw, east), (ke, west))):
        cp = pltpu.make_async_remote_copy(
            src_ref=kt_ref, dst_ref=dst, send_sem=ks_sem.at[side], recv_sem=kr_sem.at[side],
            device_id={"lon": dev}, device_id_type=MESH)
        cp.start()
        kcopies.append(cp)
    xcopies = []
    for c in range(nch):
        pair = []
        for side, (dst, dev) in enumerate(((xw, east), (xe, west))):
            cp = pltpu.make_async_remote_copy(
                src_ref=x_ref.at[pl.ds(c * ch, ch)], dst_ref=dst.at[pl.ds(c * ch, ch)],
                send_sem=xs_sem.at[side, c], recv_sem=xr_sem.at[side, c],
                device_id={"lon": dev}, device_id_type=MESH)
            cp.start()
            pair.append(cp)
        xcopies.append(pair)

    xc[0] = jnp.zeros((nb, 3 * w2), BF16)
    xc[nlat + 1] = jnp.zeros((nb, 3 * w2), BF16)
    t1[0] = jnp.zeros((nb, 2 * w2), BF16)
    t1[nlat + 1] = jnp.zeros((nb, 2 * w2), BF16)

    rows = lax.broadcasted_iota(jnp.int32, (nb, nb), 0)
    cols = lax.broadcasted_iota(jnp.int32, (nb, nb), 1)
    swap = (rows + 1 - 2 * (rows % 2) == cols).astype(F32).astype(BF16)
    lane_hi = (lax.broadcasted_iota(jnp.int32, (nb, w2), 1) >= nb).astype(jnp.int32)
    keep = lax.broadcasted_iota(jnp.int32, (nb, w2), 0) % 2 == lane_hi

    def turned(v):
        other = jnp.dot(swap, v, preferred_element_type=F32)
        return jnp.where(keep, v.astype(F32), pltpu.roll(other, nb, 1)).astype(BF16)

    def turn_own(i, carry):
        xc[i + 1, :, w2:2 * w2] = turned(x_ref[i])
        return carry

    lax.fori_loop(0, nlat, turn_own, 0, unroll=4)

    def turn_sides(i, carry):
        xc[i + 1, :, 0:w2] = turned(xw[i])
        xc[i + 1, :, 2 * w2:3 * w2] = turned(xe[i])
        return carry

    c_copy.wait()

    def widen(i, carry):
        wc[i] = jnp.concatenate(
            [coup[i, pl.ds(3 * a, 3)].reshape(3 * nb, nb) for a in range(3)], axis=1)
        return carry

    lax.fori_loop(0, nlat, widen, 0, unroll=2)

    for cp in kcopies:
        cp.wait()
    kwv, kov, kev = (jnp.transpose(v[...]) for v in (kw, kt_ref, ke))
    low = lax.broadcasted_iota(jnp.int32, (nb, w2), 1) < nb

    def spread(v, j):
        return jnp.broadcast_to(v[:, j:j + 1], (nb, w2))

    for i in range(nlat):
        kx[i, :, 0:w2] = spread(kwv, 2 * i + 1)
        kx[i, :, w2:2 * w2] = jnp.where(low, spread(kov, 2 * i), spread(kov, 2 * i + 1))
        kx[i, :, 2 * w2:3 * w2] = spread(kev, 2 * i)

    fw[...] = jnp.concatenate([foot_w_ref[k] for k in range(nk)], axis=1)
    ones = jnp.ones((8, nb), BF16)
    bin_ids = lax.broadcasted_iota(jnp.int32, (1, LANES), 1)
    for f in range(nobs):
        hot[f:f + 1] = (bin_ids == bins_ref[f]).astype(F32)

    c0, c1, c2 = coef_ref[0], coef_ref[1], coef_ref[2]

    def first(i, carry):
        p = jnp.dot(wc[i], xc[pl.ds(i, 3)].reshape(3 * nb, 3 * w2), preferred_element_type=F32)
        centre = xc[i + 1].astype(F32)
        mid = p[nb:2 * nb] + kx[i] * centre
        total = p[0:nb, 0:2 * w2] + p[2 * nb:3 * nb, w2:3 * w2] + mid[:, nb:nb + 2 * w2]
        t1[i + 1] = total.astype(BF16)
        return carry

    def second(i, carry):
        p = jnp.dot(wc[i], t1[pl.ds(i, 3)].reshape(3 * nb, 2 * w2), preferred_element_type=F32)
        own = t1[i + 1].astype(F32)[:, nb:nb + w2]
        st = (p[0:nb, 0:w2] + p[2 * nb:3 * nb, w2:2 * w2] + p[nb:2 * nb, nb:nb + w2]
              + kx[i, :, w2:2 * w2] * own)
        x = xc[i + 1, :, w2:2 * w2].astype(F32)
        f = (c0 * x + c1 * own + c2 * (2.0 * st - x)).astype(BF16)
        fown[i] = f
        fb[2 * i] = f[:, 0:nb]
        fb[2 * i + 1] = f[:, nb:w2]
        return carry

    fcopies = []
    for c in range(nch):
        for cp in xcopies[c]:
            cp.wait_recv()
        last = c == nch - 1
        t_lo, t_hi = max(c * ch - 1, 0), nlat if last else (c + 1) * ch - 1
        f_lo, f_hi = max(c * ch - 2, 0), nlat if last else (c + 1) * ch - 2
        lax.fori_loop(c * ch, (c + 1) * ch, turn_sides, 0, unroll=2)
        lax.fori_loop(t_lo, t_hi, first, 0, unroll=2)
        lax.fori_loop(f_lo, f_hi, second, 0, unroll=2)
        cp = pltpu.make_async_remote_copy(
            src_ref=fown.at[pl.ds(f_lo, f_hi - f_lo)], dst_ref=feast.at[pl.ds(f_lo, f_hi - f_lo)],
            send_sem=fs_sem.at[c], recv_sem=fr_sem.at[c],
            device_id={"lon": west}, device_id_type=MESH)
        cp.start()
        fcopies.append((cp, f_lo, f_hi))

    def turn_out(i, carry):
        filt_ref[i] = turned(fown[i])
        return carry

    lax.fori_loop(0, nlat, turn_out, 0, unroll=4)

    def unpack(i, carry):
        f = feast[i]
        fb[2 * (nlat + i)] = f[:, 0:nb]
        fb[2 * (nlat + i) + 1] = f[:, nb:w2]
        return carry

    for cp, f_lo, f_hi in fcopies:
        cp.wait_recv()
        lax.fori_loop(f_lo, f_hi, unpack, 0, unroll=2)

    nt = (((1,), (1,)), ((), ()))

    def foot(f, carry):
        picks = []
        for k in range(nk):
            la, lo = lat_ref[k, f], lon_ref[k, f]
            picks.append(fb[(lo // 2) * (2 * nlat) + 2 * la + lo % 2])
        y = jnp.dot(fw[...], jnp.concatenate(picks, axis=0), preferred_element_type=F32)
        s = jnp.tanh((thr_ref[bins_ref[f]] - y) * (0.5 / tau_width))
        hi = s.astype(BF16)
        lo_part = (s - hi.astype(F32)).astype(BF16)
        row = (lax.dot_general(ones, hi, nt, preferred_element_type=F32)
               + lax.dot_general(ones, lo_part, nt, preferred_element_type=F32))
        ecdf[pl.ds(f, 1)] = 0.5 + (0.5 / nb) * row[0:1]
        return carry

    lax.fori_loop(0, nobs, foot, 0, unroll=4)

    onehot = hot[...]
    ec = ecdf[...]
    totals = jnp.sum(onehot * jnp.sum(ec, axis=1, keepdims=True), axis=0, keepdims=True)
    counts = jnp.sum(onehot, axis=0, keepdims=True) * nb
    msg[0:1] = totals
    msg[1:2] = counts
    msg[2:8] = jnp.zeros((6, LANES), F32)
    inbox[pl.ds(me, 1)] = msg[...][None]

    def tell(off, carry):
        pltpu.make_async_remote_copy(
            src_ref=msg, dst_ref=inbox.at[me], send_sem=ms_sem.at[off], recv_sem=mr_sem.at[me],
            device_id={"lon": lax.rem(me + off, n)}, device_id_type=MESH).start()
        return carry

    lax.fori_loop(1, n, tell, 0)

    def hear(off, carry):
        src = lax.rem(me + off, n)
        pltpu.make_async_remote_copy(
            src_ref=msg, dst_ref=inbox.at[src], send_sem=ms_sem.at[off], recv_sem=mr_sem.at[src],
            device_id={"lon": src}, device_id_type=MESH).wait()
        return carry

    lax.fori_loop(1, n, hear, 0)
    allsum = jnp.sum(inbox[...], axis=0)
    summary = allsum[0:1] / jnp.maximum(allsum[1:2], 1.0)
    summ_ref[...] = summary
    score_ref[...] = ec - jnp.sum(onehot * summary, axis=1, keepdims=True)

    for pair in xcopies:
        for cp in pair:
            cp.wait_send()
    for cp, _, _ in fcopies:
        cp.wait_send()


def local(n, fields, couplings, kappa, coeffs, foot_lat, foot_lon, foot_w, thresholds, bins):
    nlat, width = fields.shape[0], fields.shape[1]
    nb = couplings.shape[-1]
    nobs, nk = foot_lat.shape
    nbins = thresholds.shape[0]
    w2 = 2 * nb
    nch = 4
    halves = nb * nb // w2
    x = fields.reshape(nlat, width, halves, w2).transpose(0, 2, 1, 3).reshape(nlat, nb, w2)
    kt = kappa.reshape(nlat * width, nb)
    vmem = pl.BlockSpec(memory_space=pltpu.VMEM)
    smem = pl.BlockSpec(memory_space=pltpu.SMEM)
    hbm = pl.BlockSpec(memory_space=pltpu.HBM)
    dma = pltpu.SemaphoreType.DMA
    filt, score, summ = pl.pallas_call(
        functools.partial(kernel, n, nlat, nb, nobs, nk, nbins, nch),
        out_shape=(
            jax.ShapeDtypeStruct((nlat, nb, w2), BF16),
            jax.ShapeDtypeStruct((nobs, nb), F32),
            jax.ShapeDtypeStruct((1, LANES), F32),
        ),
        in_specs=[vmem, vmem, hbm, vmem, smem, smem, smem, smem, smem],
        out_specs=(vmem, vmem, vmem),
        scratch_shapes=[
            pltpu.VMEM((nlat, nb, w2), BF16),
            pltpu.VMEM((nlat, nb, w2), BF16),
            pltpu.VMEM((nlat + 2, nb, 3 * w2), BF16),
            pltpu.VMEM((nlat * width, nb), F32),
            pltpu.VMEM((nlat * width, nb), F32),
            pltpu.VMEM(couplings.shape, BF16),
            pltpu.VMEM((nlat, 3 * nb, 3 * nb), BF16),
            pltpu.VMEM((nlat, nb, 3 * w2), F32),
            pltpu.VMEM((nlat + 2, nb, 2 * w2), BF16),
            pltpu.VMEM((nlat, nb, w2), BF16),
            pltpu.VMEM((nlat, nb, w2), BF16),
            pltpu.VMEM((4 * nlat, nb, nb), BF16),
            pltpu.VMEM((nb, nk * nb), BF16),
            pltpu.VMEM((nobs, LANES), F32),
            pltpu.VMEM((nobs, nb), F32),
            pltpu.VMEM((8, LANES), F32),
            pltpu.VMEM((n, 8, LANES), F32),
            dma((2, nch)), dma((2, nch)), dma((2,)), dma((2,)), dma,
            dma((nch,)), dma((nch,)), dma((n,)), dma((n,)),
        ],
        compiler_params=pltpu.CompilerParams(
            collective_id=0, has_side_effects=True, vmem_limit_bytes=50 * 1024 * 1024),
    )(x, kt, couplings, foot_w, coeffs, foot_lat.T, foot_lon.T, thresholds, bins)
    filtered = filt.reshape(nlat, halves, width, w2).transpose(0, 2, 1, 3).reshape(nlat, width, nb * nb)
    return filtered, score, summ[0, :nbins]


def solution(mesh):
    placed = (
        P("groups", "lon", None),
        P(),
        P("groups", "lon", None),
        P(),
        P(("groups", "lon"), None),
        P(("groups", "lon"), None),
        P(),
        P(),
        P(("groups", "lon")),
    )
    return jax.shard_map(
        functools.partial(local, mesh.shape["lon"]),
        mesh=mesh,
        in_specs=placed,
        out_specs=(P("groups", "lon", None), P(("groups", "lon"), None), P("groups")),
        check_vma=False,
    )
```

```python
import functools

import jax
import jax.numpy as jnp
from jax import lax
from jax.experimental import pallas as pl
from jax.experimental.pallas import tpu as pltpu
from jax.sharding import PartitionSpec as P

MESH = pl.DeviceIdType.MESH
F32 = jnp.float32
BF16 = jnp.bfloat16
tau_width = 0.5
LANES = 128


def kernel(n, nlat, nb, nobs, nk, nbins, nch, *refs):
    (x_ref, kt_ref, coup_hbm, foot_w_ref, coef_ref, lat_ref, lon_ref, thr_ref, bins_ref,
     filt_ref, score_ref, summ_ref,
     xw, xe, xc, kw, ke, coup, wc, kx, t1, fown, feast, fb, fw, hot, ecdf, msg, inbox,
     xs_sem, xr_sem, ks_sem, kr_sem, c_sem, fs_sem, fr_sem, ms_sem, mr_sem) = refs
    me = lax.axis_index("lon")
    east, west = lax.rem(me + 1, n), lax.rem(me + n - 1, n)
    ch = nlat // nch
    w2 = 2 * nb

    barrier = pltpu.get_barrier_semaphore()

    def greet(off, carry):
        pl.semaphore_signal(barrier, inc=1, device_id={"lon": lax.rem(me + off, n)}, device_id_type=MESH)
        return carry

    lax.fori_loop(1, n, greet, 0)
    c_copy = pltpu.make_async_copy(coup_hbm, coup, c_sem)
    c_copy.start()
    pl.semaphore_wait(barrier, n - 1)

    kcopies = []
    for side, (dst, dev) in enumerate(((kw, east), (ke, west))):
        cp = pltpu.make_async_remote_copy(
            src_ref=kt_ref, dst_ref=dst, send_sem=ks_sem.at[side], recv_sem=kr_sem.at[side],
            device_id={"lon": dev}, device_id_type=MESH)
        cp.start()
        kcopies.append(cp)
    xcopies = []
    for c in range(nch):
        pair = []
        for side, (dst, dev) in enumerate(((xw, east), (xe, west))):
            cp = pltpu.make_async_remote_copy(
                src_ref=x_ref.at[pl.ds(c * ch, ch)], dst_ref=dst.at[pl.ds(c * ch, ch)],
                send_sem=xs_sem.at[side, c], recv_sem=xr_sem.at[side, c],
                device_id={"lon": dev}, device_id_type=MESH)
            cp.start()
            pair.append(cp)
        xcopies.append(pair)

    xc[0] = jnp.zeros((nb, 3 * w2), BF16)
    xc[nlat + 1] = jnp.zeros((nb, 3 * w2), BF16)
    t1[0] = jnp.zeros((nb, 2 * w2), BF16)
    t1[nlat + 1] = jnp.zeros((nb, 2 * w2), BF16)

    rows = lax.broadcasted_iota(jnp.int32, (nb, nb), 0)
    cols = lax.broadcasted_iota(jnp.int32, (nb, nb), 1)
    swap = (rows + 1 - 2 * (rows % 2) == cols).astype(F32).astype(BF16)
    lane_hi = (lax.broadcasted_iota(jnp.int32, (nb, w2), 1) >= nb).astype(jnp.int32)
    keep = lax.broadcasted_iota(jnp.int32, (nb, w2), 0) % 2 == lane_hi

    def turned(v):
        other = jnp.dot(swap, v, preferred_element_type=F32)
        return jnp.where(keep, v.astype(F32), pltpu.roll(other, nb, 1)).astype(BF16)

    def turn_own(i, carry):
        xc[i + 1, :, w2:2 * w2] = turned(x_ref[i])
        return carry

    lax.fori_loop(0, nlat, turn_own, 0, unroll=4)

    def turn_sides(i, carry):
        xc[i + 1, :, 0:w2] = turned(xw[i])
        xc[i + 1, :, 2 * w2:3 * w2] = turned(xe[i])
        return carry

    c_copy.wait()

    def widen(i, carry):
        wc[i] = jnp.concatenate(
            [coup[i, pl.ds(3 * a, 3)].reshape(3 * nb, nb) for a in range(3)], axis=1)
        return carry

    lax.fori_loop(0, nlat, widen, 0, unroll=2)

    for cp in kcopies:
        cp.wait()
    kwv, kov, kev = (jnp.transpose(v[...]) for v in (kw, kt_ref, ke))
    low = lax.broadcasted_iota(jnp.int32, (nb, w2), 1) < nb

    def spread(v, j):
        return jnp.broadcast_to(v[:, j:j + 1], (nb, w2))

    for i in range(nlat):
        kx[i, :, 0:w2] = spread(kwv, 2 * i + 1)
        kx[i, :, w2:2 * w2] = jnp.where(low, spread(kov, 2 * i), spread(kov, 2 * i + 1))
        kx[i, :, 2 * w2:3 * w2] = spread(kev, 2 * i)

    fw[...] = jnp.concatenate([foot_w_ref[k] for k in range(nk)], axis=1)
    ones = jnp.ones((8, nb), BF16)
    bin_ids = lax.broadcasted_iota(jnp.int32, (1, LANES), 1)
    for f in range(nobs):
        hot[f:f + 1] = (bin_ids == bins_ref[f]).astype(F32)

    c0, c1, c2 = coef_ref[0], coef_ref[1], coef_ref[2]

    def first(i, carry):
        p = jnp.dot(wc[i], xc[pl.ds(i, 3)].reshape(3 * nb, 3 * w2), preferred_element_type=F32)
        centre = xc[i + 1].astype(F32)
        mid = p[nb:2 * nb] + kx[i] * centre
        total = p[0:nb, 0:2 * w2] + p[2 * nb:3 * nb, w2:3 * w2] + mid[:, nb:nb + 2 * w2]
        t1[i + 1] = total.astype(BF16)
        return carry

    def second(i, carry):
        p = jnp.dot(wc[i], t1[pl.ds(i, 3)].reshape(3 * nb, 2 * w2), preferred_element_type=F32)
        own = t1[i + 1].astype(F32)[:, nb:nb + w2]
        st = (p[0:nb, 0:w2] + p[2 * nb:3 * nb, w2:2 * w2] + p[nb:2 * nb, nb:nb + w2]
              + kx[i, :, w2:2 * w2] * own)
        x = xc[i + 1, :, w2:2 * w2].astype(F32)
        f = (c0 * x + c1 * own + c2 * (2.0 * st - x)).astype(BF16)
        fown[i] = f
        fb[2 * i] = f[:, 0:nb]
        fb[2 * i + 1] = f[:, nb:w2]
        return carry

    fcopies = []
    for c in range(nch):
        for cp in xcopies[c]:
            cp.wait_recv()
        last = c == nch - 1
        t_lo, t_hi = max(c * ch - 1, 0), nlat if last else (c + 1) * ch - 1
        f_lo, f_hi = max(c * ch - 2, 0), nlat if last else (c + 1) * ch - 2
        lax.fori_loop(c * ch, (c + 1) * ch, turn_sides, 0, unroll=4)
        lax.fori_loop(t_lo, t_hi, first, 0, unroll=4)
        lax.fori_loop(f_lo, f_hi, second, 0, unroll=4)
        cp = pltpu.make_async_remote_copy(
            src_ref=fown.at[pl.ds(f_lo, f_hi - f_lo)], dst_ref=feast.at[pl.ds(f_lo, f_hi - f_lo)],
            send_sem=fs_sem.at[c], recv_sem=fr_sem.at[c],
            device_id={"lon": west}, device_id_type=MESH)
        cp.start()
        fcopies.append((cp, f_lo, f_hi))

    def turn_out(i, carry):
        filt_ref[i] = turned(fown[i])
        return carry

    lax.fori_loop(0, nlat, turn_out, 0, unroll=4)

    def unpack(i, carry):
        f = feast[i]
        fb[2 * (nlat + i)] = f[:, 0:nb]
        fb[2 * (nlat + i) + 1] = f[:, nb:w2]
        return carry

    for cp, f_lo, f_hi in fcopies:
        cp.wait_recv()
        lax.fori_loop(f_lo, f_hi, unpack, 0, unroll=2)

    nt = (((1,), (1,)), ((), ()))

    def foot(f, carry):
        picks = []
        for k in range(nk):
            la, lo = lat_ref[k, f], lon_ref[k, f]
            picks.append(fb[(lo // 2) * (2 * nlat) + 2 * la + lo % 2])
        y = jnp.dot(fw[...], jnp.concatenate(picks, axis=0), preferred_element_type=F32)
        s = jnp.tanh((thr_ref[bins_ref[f]] - y) * (0.5 / tau_width))
        hi = s.astype(BF16)
        lo_part = (s - hi.astype(F32)).astype(BF16)
        row = (lax.dot_general(ones, hi, nt, preferred_element_type=F32)
               + lax.dot_general(ones, lo_part, nt, preferred_element_type=F32))
        ecdf[pl.ds(f, 1)] = 0.5 + (0.5 / nb) * row[0:1]
        return carry

    lax.fori_loop(0, nobs, foot, 0, unroll=8)

    onehot = hot[...]
    ec = ecdf[...]
    totals = jnp.sum(onehot * jnp.sum(ec, axis=1, keepdims=True), axis=0, keepdims=True)
    counts = jnp.sum(onehot, axis=0, keepdims=True) * nb
    msg[0:1] = totals
    msg[1:2] = counts
    msg[2:8] = jnp.zeros((6, LANES), F32)
    inbox[pl.ds(me, 1)] = msg[...][None]

    def tell(off, carry):
        pltpu.make_async_remote_copy(
            src_ref=msg, dst_ref=inbox.at[me], send_sem=ms_sem.at[off], recv_sem=mr_sem.at[me],
            device_id={"lon": lax.rem(me + off, n)}, device_id_type=MESH).start()
        return carry

    lax.fori_loop(1, n, tell, 0)

    def hear(off, carry):
        src = lax.rem(me + off, n)
        pltpu.make_async_remote_copy(
            src_ref=msg, dst_ref=inbox.at[src], send_sem=ms_sem.at[off], recv_sem=mr_sem.at[src],
            device_id={"lon": src}, device_id_type=MESH).wait()
        return carry

    lax.fori_loop(1, n, hear, 0)
    allsum = jnp.sum(inbox[...], axis=0)
    summary = allsum[0:1] / jnp.maximum(allsum[1:2], 1.0)
    summ_ref[...] = summary
    score_ref[...] = ec - jnp.sum(onehot * summary, axis=1, keepdims=True)

    for pair in xcopies:
        for cp in pair:
            cp.wait_send()
    for cp, _, _ in fcopies:
        cp.wait_send()


def local(n, fields, couplings, kappa, coeffs, foot_lat, foot_lon, foot_w, thresholds, bins):
    nlat, width = fields.shape[0], fields.shape[1]
    nb = couplings.shape[-1]
    nobs, nk = foot_lat.shape
    nbins = thresholds.shape[0]
    w2 = 2 * nb
    nch = 8
    halves = nb * nb // w2
    x = fields.reshape(nlat, width, halves, w2).transpose(0, 2, 1, 3).reshape(nlat, nb, w2)
    kt = kappa.reshape(nlat * width, nb)
    vmem = pl.BlockSpec(memory_space=pltpu.VMEM)
    smem = pl.BlockSpec(memory_space=pltpu.SMEM)
    hbm = pl.BlockSpec(memory_space=pltpu.HBM)
    dma = pltpu.SemaphoreType.DMA
    filt, score, summ = pl.pallas_call(
        functools.partial(kernel, n, nlat, nb, nobs, nk, nbins, nch),
        out_shape=(
            jax.ShapeDtypeStruct((nlat, nb, w2), BF16),
            jax.ShapeDtypeStruct((nobs, nb), F32),
            jax.ShapeDtypeStruct((1, LANES), F32),
        ),
        in_specs=[vmem, vmem, hbm, vmem, smem, smem, smem, smem, smem],
        out_specs=(vmem, vmem, vmem),
        scratch_shapes=[
            pltpu.VMEM((nlat, nb, w2), BF16),
            pltpu.VMEM((nlat, nb, w2), BF16),
            pltpu.VMEM((nlat + 2, nb, 3 * w2), BF16),
            pltpu.VMEM((nlat * width, nb), F32),
            pltpu.VMEM((nlat * width, nb), F32),
            pltpu.VMEM(couplings.shape, BF16),
            pltpu.VMEM((nlat, 3 * nb, 3 * nb), BF16),
            pltpu.VMEM((nlat, nb, 3 * w2), F32),
            pltpu.VMEM((nlat + 2, nb, 2 * w2), BF16),
            pltpu.VMEM((nlat, nb, w2), BF16),
            pltpu.VMEM((nlat, nb, w2), BF16),
            pltpu.VMEM((4 * nlat, nb, nb), BF16),
            pltpu.VMEM((nb, nk * nb), BF16),
            pltpu.VMEM((nobs, LANES), F32),
            pltpu.VMEM((nobs, nb), F32),
            pltpu.VMEM((8, LANES), F32),
            pltpu.VMEM((n, 8, LANES), F32),
            dma((2, nch)), dma((2, nch)), dma((2,)), dma((2,)), dma,
            dma((nch,)), dma((nch,)), dma((n,)), dma((n,)),
        ],
        compiler_params=pltpu.CompilerParams(
            collective_id=0, has_side_effects=True, vmem_limit_bytes=50 * 1024 * 1024),
    )(x, kt, couplings, foot_w, coeffs, foot_lat.T, foot_lon.T, thresholds, bins)
    filtered = filt.reshape(nlat, halves, width, w2).transpose(0, 2, 1, 3).reshape(nlat, width, nb * nb)
    return filtered, score, summ[0, :nbins]


def solution(mesh):
    placed = (
        P("groups", "lon", None),
        P(),
        P("groups", "lon", None),
        P(),
        P(("groups", "lon"), None),
        P(("groups", "lon"), None),
        P(),
        P(),
        P(("groups", "lon")),
    )
    return jax.shard_map(
        functools.partial(local, mesh.shape["lon"]),
        mesh=mesh,
        in_specs=placed,
        out_specs=(P("groups", "lon", None), P(("groups", "lon"), None), P("groups")),
        check_vma=False,
    )
```
